32 devices in a mesh: groups: 2 (over x), rows: 16 (over z, y, core).
Axes of the slice: x: 2, y: 2, z: 4, core: 2. Of those that a mesh axis runs over, the one named last changes fastest.
Arguments:
- samples: bfloat16 [32768, 256], P(('groups', 'rows')), parts along dimension 0
- omega_diag: float32 [256, 128, 128], P(('groups', 'rows')), parts along dimension 0, as said below
- omega_off: float32 [960, 128, 128], P(('groups', 'rows')), parts along dimension 0, as said below
- pattern: int32 [960, 2], P(('groups', 'rows')), parts along dimension 0, may hold values from 0 to 127, as said below
- block_count: int32 [256], P(('groups', 'rows')), parts along dimension 0, may hold values from 0 to 15, as said below
- diag_term: float32 [32768], P(('groups', 'rows')), parts along dimension 0, may hold values from -1 to -0.5
Outputs:
- omega_diag_next: float32 [256, 128, 128], P(('groups', 'rows')), parts along dimension 0
- omega_off_next: float32 [960, 128, 128], P(('groups', 'rows')), parts along dimension 0
- objective: float32 [2], P('groups'), parts along dimension 0
The draws below stay inside these ranges and needn't reach their ends.
There are 2 independent parts, one for each index of `groups`. The reference program is written for one: setup_inputs(seed, part) draws one part's arguments, and reference() takes and returns one part's arrays. A program takes and returns all parts, laid end to end along the dimension named above; each array names one. Nothing has to cross between parts.
Inputs may be any that keep to these rules, and one draw needn't show every extreme that they name: `pattern`: row e names a stored off-diagonal block by its block row i, which lies on the device holding e, and its block column j; for live entries j lies on another device. A device's live entries come first, ordered by block row; the live entries of all devices are symmetric: (j, i) is live wherever (i, j) is, and no pair is named twice. Between the block rows of two devices there are either none or exactly 2 live blocks. Dead entries name the device's first block row twice. The live entries of a device are its first entries, as many as the sum of block_count over its 8 block rows; some device has all 30 entries live. `omega_diag`: each diagonal block is symmetric. Omega is symmetric: for live entries e = (i, j) and f = (j, i), omega_off[f] is the transpose of omega_off[e].
All inputs are finite; a program needn't handle non-finite values.
Results may differ from the reference program's by a relative error of at most 0.0003.
Values may be sent and summed in bfloat16 or wider, within the bound.
A program may use at most 128 MiB of HBM per device.

```python
import jax
import jax.numpy as jnp
from jax import lax

BLOCK = 128
BR_DEV = 8
SAMPLES = 256
NEAR = 3
LINKS = 15
ENTRIES = 30
BLOCK_ROWS = 128
VARIABLES = 16384
N_ROWS = 16


def pattern_tables(key):
    streams = jax.random.split(jax.random.fold_in(key, 11), 5)
    half_axis = N_ROWS // 2
    pool = jax.random.permutation(streams[0], N_ROWS - 2 - NEAR)[:LINKS - NEAR - 1].astype(jnp.int32) + NEAR + 1
    distant = jnp.where(pool >= half_axis, pool + 1, pool)
    offsets = jnp.concatenate([jnp.arange(1, NEAR + 1, dtype=jnp.int32), jnp.full((1,), half_axis, jnp.int32), distant])
    row_flip = jax.random.randint(streams[1], (LINKS,), 1, BR_DEV, dtype=jnp.int32)
    anchor = jax.random.randint(streams[2], (), 0, BR_DEV, dtype=jnp.int32)
    busiest = jax.random.randint(streams[3], (), 0, N_ROWS, dtype=jnp.int32)
    chance = jax.random.randint(streams[4], (N_ROWS, LINKS), 0, 4, dtype=jnp.int32)
    devices = jnp.broadcast_to(jnp.arange(N_ROWS, dtype=jnp.int32)[:, None], (N_ROWS, LINKS))
    lane_ids = jnp.broadcast_to(jnp.arange(LINKS, dtype=jnp.int32)[None, :], (N_ROWS, LINKS))
    partner = jnp.bitwise_xor(devices, offsets[None, :])
    smaller = jnp.minimum(devices, partner)
    active = (lane_ids <= NEAR) | (devices == busiest) | (partner == busiest) | (chance[smaller, lane_ids] < 3)
    flipped = jnp.broadcast_to(jnp.bitwise_xor(anchor, row_flip)[None, :], (N_ROWS, LINKS))
    rows_first = devices * BR_DEV + anchor
    cols_first = partner * BR_DEV + flipped
    rows_second = devices * BR_DEV + flipped
    cols_second = partner * BR_DEV + anchor
    own_first = devices * ENTRIES + 2 * lane_ids
    mate_first = partner * ENTRIES + 2 * lane_ids + 1
    own_second = devices * ENTRIES + 2 * lane_ids + 1
    mate_second = partner * ENTRIES + 2 * lane_ids
    lower = devices < partner
    source_first = jnp.where(lower, own_first, mate_first)
    source_second = jnp.where(lower, own_second, mate_second)
    row_ids = jnp.stack([rows_first, rows_second], axis=2).reshape(N_ROWS, ENTRIES)
    col_ids = jnp.stack([cols_first, cols_second], axis=2).reshape(N_ROWS, ENTRIES)
    valid = jnp.stack([active, active], axis=2).reshape(N_ROWS, ENTRIES)
    sources = jnp.stack([source_first, source_second], axis=2).reshape(N_ROWS, ENTRIES)
    turned = jnp.stack([~lower, ~lower], axis=2).reshape(N_ROWS, ENTRIES)
    base_rows = devices[:, :1] * BR_DEV
    slot_ids = jnp.arange(ENTRIES, dtype=jnp.int32)[None, :]
    scores = jnp.where(valid, (row_ids - base_rows) * ENTRIES + slot_ids, BR_DEV * ENTRIES + slot_ids)
    ordering = jnp.argsort(scores, axis=1)
    row_ids = jnp.take_along_axis(row_ids, ordering, axis=1)
    col_ids = jnp.take_along_axis(col_ids, ordering, axis=1)
    valid = jnp.take_along_axis(valid, ordering, axis=1)
    sources = jnp.take_along_axis(sources, ordering, axis=1)
    turned = jnp.take_along_axis(turned, ordering, axis=1)
    row_ids = jnp.where(valid, row_ids, base_rows)
    col_ids = jnp.where(valid, col_ids, base_rows)
    pattern = jnp.stack([row_ids, col_ids], axis=2).reshape(N_ROWS * ENTRIES, 2)
    row_counts = jnp.zeros((BR_DEV * N_ROWS,), jnp.int32).at[row_ids.reshape(-1)].add(valid.reshape(-1).astype(jnp.int32))
    return (pattern, row_counts, sources.reshape(-1), turned.reshape(-1))


def draw_pattern(key, part):
    return pattern_tables(key)[0]


def draw_block_count(key, part):
    return pattern_tables(key)[1]


def draw_omega_off(key, part):
    tables = pattern_tables(key)
    sources = tables[2]
    turned = tables[3]
    extent = (N_ROWS * ENTRIES, BLOCK, BLOCK)
    raw = jnp.clip(jax.random.normal(jax.random.fold_in(key, 23), extent, jnp.float32) * 0.05, -0.3, 0.3)
    chosen = raw[sources]
    return jnp.where(turned[:, None, None], jnp.swapaxes(chosen, 1, 2), chosen)


def draw_samples(key, part):
    rows_pos = jnp.arange(VARIABLES, dtype=jnp.float32)[:, None] / VARIABLES
    spread = jnp.sqrt(1.0 + 2.0 * rows_pos)
    values = jax.random.normal(key, (VARIABLES, SAMPLES), jnp.float32)
    return (values * spread).astype(jnp.bfloat16)


def draw_omega_diag(key, part):
    first, second = jax.random.split(key)
    extent = (BLOCK_ROWS, BLOCK, BLOCK)
    identity = jnp.eye(BLOCK, dtype=jnp.float32)[None]
    spread = jax.random.uniform(first, extent, jnp.float32, 1.0, 2.0)
    noise = jax.random.normal(second, extent, jnp.float32)
    coupling = jnp.clip((noise + jnp.swapaxes(noise, 1, 2)) * 0.0354, -0.3, 0.3)
    return identity * spread + (1.0 - identity) * coupling


def block_scale(key, dims, shards, smallest, largest):
    def one(axis_at, parts):
        heights = jax.random.uniform(jax.random.fold_in(jax.random.fold_in(key, 6), axis_at), (parts,), jnp.float32, smallest / len(shards), largest / len(shards))
        return jnp.repeat(jnp.exp(heights), dims[axis_at] // parts).reshape((-1,) + (1,) * (len(dims) - axis_at - 1))

    gain = one(*shards[0])
    for cut in shards[1:]:
        gain = gain * one(*cut)
    return gain


def setup_inputs(seed: int = 0, part: int = 0) -> dict:
    arg_keys = jax.random.split(jax.random.key(seed), 7)
    part_splits = jax.random.split(jax.random.fold_in(arg_keys[6], part), 7)
    return {
        "samples": draw_samples(jax.random.fold_in(jax.random.fold_in(arg_keys[6], part), 71), part),
        "omega_diag": draw_omega_diag(jax.random.fold_in(jax.random.fold_in(arg_keys[6], part), 71), part),
        "omega_off": draw_omega_off(jax.random.fold_in(jax.random.fold_in(arg_keys[6], part), 71), part),
        "pattern": draw_pattern(jax.random.fold_in(jax.random.fold_in(arg_keys[6], part), 71), part),
        "block_count": draw_block_count(jax.random.fold_in(jax.random.fold_in(arg_keys[6], part), 71), part),
        "diag_term": jnp.clip(-1.0 + 0.5 * jax.random.uniform(part_splits[5], (VARIABLES,), jnp.float32) ** block_scale(part_splits[5], (VARIABLES,), ((0, 16),), -0.2, 0.2), -1.0, -0.5),
    }


STEP_SIZE = 0.5
PENALTY = 0.01


def soften(values, level):
    return values - jnp.clip(values, -level, level)


def reference(samples, omega_diag, omega_off, pattern, block_count, diag_term):
    highest = lax.Precision.HIGHEST
    block_total = BR_DEV * N_ROWS
    entry_total = ENTRIES * N_ROWS
    xblocks = samples.astype(jnp.float32).reshape(block_total, BLOCK, SAMPLES)
    positions = jnp.arange(entry_total, dtype=jnp.int32)
    per_device = jnp.sum(block_count.reshape(N_ROWS, BR_DEV), axis=1)
    living = (positions % ENTRIES) < per_device[positions // ENTRIES]
    row_ids = pattern[:, 0]
    col_ids = pattern[:, 1]
    masked = jnp.where(living[:, None, None], omega_off, 0.0)
    projected = jnp.einsum("kab,kbn->kan", omega_diag, xblocks, precision=highest)
    device_ids = jnp.arange(N_ROWS, dtype=jnp.int32)

    def add_device(carry, device):
        start = device * ENTRIES
        blocks = lax.dynamic_slice_in_dim(masked, start, ENTRIES, 0)
        targets = lax.dynamic_slice_in_dim(row_ids, start, ENTRIES, 0)
        sources = lax.dynamic_slice_in_dim(col_ids, start, ENTRIES, 0)
        contributions = jnp.einsum("eab,ebn->ean", blocks, xblocks[sources], precision=highest)
        return carry + jax.ops.segment_sum(contributions, targets, num_segments=block_total), None

    projected = lax.scan(add_device, projected, device_ids)[0]

    def products(device):
        start = device * ENTRIES
        targets = lax.dynamic_slice_in_dim(row_ids, start, ENTRIES, 0)
        sources = lax.dynamic_slice_in_dim(col_ids, start, ENTRIES, 0)
        return jnp.einsum("ean,ebn->eab", projected[targets], xblocks[sources], precision=highest)

    off_products = lax.map(products, device_ids).reshape(entry_total, BLOCK, BLOCK)
    entry_keys = jnp.where(living, row_ids * block_total + col_ids, block_total * block_total + positions)
    ordering = jnp.argsort(entry_keys)
    located = jnp.searchsorted(entry_keys[ordering], col_ids * block_total + row_ids)
    partner = ordering[jnp.clip(located, 0, entry_total - 1)]
    mirrored = jnp.swapaxes(off_products[partner], 1, 2)
    gradient = (off_products + mirrored) / (2.0 * SAMPLES)
    off_next = jnp.where(living[:, None, None], soften(omega_off - STEP_SIZE * gradient, STEP_SIZE * PENALTY), 0.0)
    diag_products = jnp.einsum("kan,kbn->kab", projected, xblocks, precision=highest)
    identity = jnp.eye(BLOCK, dtype=jnp.float32)[None]
    diag_gradient = (diag_products + jnp.swapaxes(diag_products, 1, 2)) / (2.0 * SAMPLES) + identity * diag_term.reshape(block_total, BLOCK)[:, :, None]
    moved = omega_diag - STEP_SIZE * diag_gradient
    diag_next = jnp.where(identity > 0.5, moved, soften(moved, STEP_SIZE * PENALTY))
    objective = (jnp.sum(projected * projected) / (2.0 * SAMPLES) - jnp.sum(jnp.log(jnp.diagonal(omega_diag, axis1=1, axis2=2)))) / (block_total * BLOCK)
    return diag_next, off_next, objective.reshape(1)
```

```python
import functools

import jax
import jax.numpy as jnp
from jax import lax
from jax.experimental import pallas as pl
from jax.experimental.pallas import tpu as pltpu
from jax.sharding import PartitionSpec as P

STEP_SIZE = 0.5
PENALTY = 0.01
LEVELS = 32767.0
AXIS = "rows"


def soften(values, level):
    return values - jnp.clip(values, -level, level)


def halves(values):
    high = values.astype(jnp.bfloat16)
    low = (values - high.astype(jnp.float32)).astype(jnp.bfloat16)
    return jnp.concatenate([high, low], axis=1)


def times(left, right):
    return lax.dot_general(
        halves(left),
        jnp.concatenate([right, right], axis=0),
        (((1,), (0,)), ((), ())),
        preferred_element_type=jnp.float32,
    )


def times_turned(left, right):
    return lax.dot_general(
        halves(left),
        jnp.concatenate([right, right], axis=1),
        (((1,), (1,)), ((), ())),
        preferred_element_type=jnp.float32,
    )


def peer_of(me, step, n):
    if n & (n - 1):
        return (me + step) % n
    total = 0
    bit = 1
    while bit < n:
        total = total + bit * (((me // bit) % 2 + (step // bit) % 2) % 2)
        bit *= 2
    return total


def kernel(
    n,
    table,
    pattern,
    counts,
    samples,
    diag_hbm,
    off_hbm,
    term,
    diag_out,
    off_out,
    objective,
    diag,
    off,
    x_send,
    x_recv,
    parts,
    runs,
    q_send,
    q_recv,
    aux_send,
    aux_recv,
    last,
    logs,
    load_sems,
    out_sems,
    x_send_sems,
    x_recv_sems,
    q_send_sems,
    q_recv_sems,
    aux_send_sems,
    aux_recv_sems,
):
    me = lax.axis_index(AXIS)
    rows, edge = diag.shape[0], diag.shape[1]
    entries = off.shape[0]
    columns = samples.shape[2]
    width = 2.0 * columns

    load_diag = pltpu.make_async_copy(diag_hbm, diag, load_sems.at[0])
    load_off = pltpu.make_async_copy(off_hbm, off, load_sems.at[1])
    load_diag.start()
    load_off.start()

    barrier = pltpu.get_barrier_semaphore()

    def greet(i, carry):
        pl.semaphore_signal(
            barrier,
            inc=1,
            device_id={AXIS: peer_of(me, n - 1 - i, n)},
            device_id_type=pl.DeviceIdType.MESH,
        )
        return carry

    lax.fori_loop(0, n - 1, greet, 0)

    def remote(source, target, send_sems, recv_sems, peer, mine):
        return pltpu.make_async_remote_copy(
            src_ref=source.at[peer],
            dst_ref=target.at[mine],
            send_sem=send_sems.at[peer],
            recv_sem=recv_sems.at[mine],
            device_id={AXIS: peer},
            device_id_type=pl.DeviceIdType.MESH,
        )

    x_copy = functools.partial(remote, x_send, x_recv, x_send_sems, x_recv_sems)
    q_copy = functools.partial(remote, q_send, q_recv, q_send_sems, q_recv_sems)
    aux_copy = functools.partial(
        remote, aux_send, aux_recv, aux_send_sems, aux_recv_sems
    )

    pl.semaphore_wait(barrier, n - 1)

    def send_samples(i, carry):
        peer = peer_of(me, n - 1 - i, n)
        for slot in range(2):
            entry = table[slot, peer]
            x_send[peer, slot] = samples[pattern[entry, 0] % rows]
        x_copy(peer, me).start()
        return carry

    lax.fori_loop(0, n - 1, send_samples, 0)

    eye = lax.broadcasted_iota(jnp.int32, (edge, edge), 0) == lax.broadcasted_iota(
        jnp.int32, (edge, edge), 1
    )
    identity = eye.astype(jnp.float32)

    total = jnp.int32(0)
    for r in range(rows):
        count = counts[r]
        total = total + count
        last[r] = jnp.where(count > 0, rows + total - 1, r)

    load_diag.wait()

    logs[...] = jnp.zeros_like(logs)

    def own_products(r, carry):
        block = diag[r]
        runs[r] = times(block, samples[r])
        logs[...] += jnp.log(jnp.sum(block * identity, axis=0, keepdims=True))
        return carry

    lax.fori_loop(0, rows, own_products, 0)
    load_off.wait()

    def take_samples(i, carry):
        peer = peer_of(me, n - 1 - i, n)
        x_copy(peer, peer).wait_recv()
        for slot in range(2):
            entry = table[2 + slot, peer]
            parts[peer, slot] = times(off[entry], x_recv[peer, slot])
        return carry

    lax.fori_loop(0, n - 1, take_samples, 0)

    def place(entry):
        owner = pattern[entry, 1] // rows
        return owner, jnp.where(table[3, owner] == entry, 1, 0)

    def accumulate(entry, carry):
        row = pattern[entry, 0] % rows
        before = pattern[jnp.maximum(entry - 1, 0), 0] % rows
        fresh = (entry == 0) | (row != before)
        base = jnp.where(fresh, row, rows + entry - 1)
        owner, slot = place(entry)
        part = parts[owner, slot]
        runs[rows + entry] = runs[base] + jnp.where(entry < total, part, 0.0)
        return carry

    lax.fori_loop(0, entries, accumulate, 0)

    squares = jnp.zeros((1, columns), jnp.float32)
    for r in range(rows):
        values = runs[last[r]]
        squares = squares + jnp.sum(values * values, axis=0, keepdims=True)
    lanes = -logs[...]
    for start in range(0, columns, edge):
        lanes = lanes + squares[:, start : start + edge] / width
    aux_recv[me, 2:3, :] = lanes

    def send_products(i, carry):
        peer = peer_of(me, n - 1 - i, n)
        for slot in range(2):
            entry = table[slot, peer]
            values = runs[last[pattern[entry, 0] % rows]]
            other = jnp.where(table[3, peer] == entry, 1, 0)
            product = times_turned(values, x_recv[peer, other])
            parts[peer, slot, :, :edge] = product
            largest = jnp.maximum(
                jnp.max(jnp.abs(product), axis=0, keepdims=True), 1e-30
            )
            coded = jnp.round(product * (LEVELS / largest))
            q_send[peer, slot] = coded.astype(jnp.int32).astype(jnp.int16)
            aux_send[peer, slot : slot + 1, :] = largest / LEVELS
        aux_send[peer, 2:3, :] = lanes
        aux_copy(peer, me).start()
        q_copy(peer, me).start()
        return carry

    lax.fori_loop(0, n - 1, send_products, 0)

    def finish_diag(r, carry):
        product = times_turned(runs[last[r]], samples[r])
        slope = (product + product.T) / width + identity * term[pl.ds(r, 1), :]
        moved = diag[r] - STEP_SIZE * slope
        diag_out[r] = jnp.where(eye, moved, soften(moved, STEP_SIZE * PENALTY))
        return carry

    lax.fori_loop(0, rows, finish_diag, 0)

    def take_products(i, carry):
        peer = peer_of(me, n - 1 - i, n)
        aux_copy(peer, peer).wait_recv()
        q_copy(peer, peer).wait_recv()
        for slot in range(2):
            entry = table[2 + slot, peer]
            sent = jnp.where(table[1, peer] == entry, 1, 0)
            product = parts[peer, sent][:, :edge]
            scale = aux_recv[peer, slot : slot + 1, :]
            coded = q_recv[peer, slot].astype(jnp.int32).astype(jnp.float32)
            slope = (product + (coded * scale).T) / width
            parts[peer, slot, :, edge : 2 * edge] = soften(
                off[entry] - STEP_SIZE * slope, STEP_SIZE * PENALTY
            )
        return carry

    lax.fori_loop(0, n - 1, take_products, 0)

    def store_copy(entry):
        return pltpu.make_async_copy(
            runs.at[rows + entry, :, pl.ds(0, edge)],
            off_out.at[entry],
            out_sems.at[entry],
        )

    def store_off(entry, carry):
        owner, slot = place(entry)
        values = parts[owner, slot][:, edge : 2 * edge]
        runs[rows + entry, :, :edge] = jnp.where(entry < total, values, 0.0)
        store_copy(entry).start()
        return carry

    lax.fori_loop(0, entries, store_off, 0)

    def add_lanes(d, carry):
        return carry + aux_recv[d, 2:3, :]

    lanes = lax.fori_loop(0, n, add_lanes, jnp.zeros((1, edge), jnp.float32))
    objective[...] = jnp.broadcast_to(
        jnp.sum(lanes, axis=1, keepdims=True) / (rows * n * edge), objective.shape
    )

    def drain(i, carry):
        peer = peer_of(me, n - 1 - i, n)
        x_copy(peer, me).wait_send()
        q_copy(peer, me).wait_send()
        aux_copy(peer, me).wait_send()
        return carry

    lax.fori_loop(0, n - 1, drain, 0)

    def drain_out(entry, carry):
        store_copy(entry).wait()
        return carry

    lax.fori_loop(0, entries, drain_out, 0)


def shards(samples, omega_diag, omega_off, pattern, block_count, diag_term):
    n = lax.axis_size(AXIS)
    rows, edge = omega_diag.shape[0], omega_diag.shape[1]
    columns = samples.shape[1]
    entries = omega_off.shape[0]
    blocks = rows * n
    ids = jnp.arange(entries, dtype=jnp.int32)
    living = ids < jnp.sum(block_count)
    row, col = pattern[:, 0], pattern[:, 1]
    forth = row * blocks + col
    back = col * blocks + row
    top = blocks * blocks
    keys = jnp.stack([forth, top - forth, back, top - back]) * entries + ids
    linked = living & (
        (col // rows)[None, :] == jnp.arange(n, dtype=jnp.int32)[:, None]
    )
    table = (
        jnp.min(
            jnp.where(linked[None], keys[:, None, :], (top + 1) * entries), axis=2
        )
        % entries
    )
    f32, bf16, i16 = jnp.float32, jnp.bfloat16, jnp.int16
    smem = pl.BlockSpec(memory_space=pltpu.SMEM)
    vmem = pl.BlockSpec(memory_space=pltpu.VMEM)
    hbm = pl.BlockSpec(memory_space=pl.ANY)
    dma = pltpu.SemaphoreType.DMA
    diag_next, off_next, objective = pl.pallas_call(
        functools.partial(kernel, n),
        out_shape=(
            jax.ShapeDtypeStruct(omega_diag.shape, f32),
            jax.ShapeDtypeStruct(omega_off.shape, f32),
            jax.ShapeDtypeStruct((1, edge), f32),
        ),
        in_specs=[smem, smem, smem, vmem, hbm, hbm, vmem],
        out_specs=(vmem, hbm, vmem),
        scratch_shapes=[
            pltpu.VMEM(omega_diag.shape, f32),
            pltpu.VMEM(omega_off.shape, f32),
            pltpu.VMEM((n, 2, edge, columns), bf16),
            pltpu.VMEM((n, 2, edge, columns), bf16),
            pltpu.VMEM((n, 2, edge, columns), f32),
            pltpu.VMEM((rows + entries, edge, columns), f32),
            pltpu.VMEM((n, 2, edge, edge), i16),
            pltpu.VMEM((n, 2, edge, edge), i16),
            pltpu.VMEM((n, 8, edge), f32),
            pltpu.VMEM((n, 8, edge), f32),
            pltpu.SMEM((rows,), jnp.int32),
            pltpu.VMEM((1, edge), f32),
            dma((2,)),
            dma((entries,)),
        ]
        + [dma((n,))] * 6,
        compiler_params=pltpu.CompilerParams(
            collective_id=0,
            has_side_effects=True,
            vmem_limit_bytes=60 * 1024 * 1024,
        ),
    )(
        table,
        pattern,
        block_count,
        samples.reshape(rows, edge, columns),
        omega_diag,
        omega_off,
        diag_term.reshape(rows, edge),
    )
    return diag_next, off_next, objective[0, :1]


def solution(mesh):
    return jax.shard_map(
        shards,
        mesh=mesh,
        in_specs=(
            P(("groups", "rows"), None),
            P(("groups", "rows"), None, None),
            P(("groups", "rows"), None, None),
            P(("groups", "rows"), None),
            P(("groups", "rows")),
            P(("groups", "rows")),
        ),
        out_specs=(
            P(("groups", "rows"), None, None),
            P(("groups", "rows"), None, None),
            P("groups"),
        ),
        check_vma=False,
    )
```

```python
import functools

import jax
import jax.numpy as jnp
from jax import lax
from jax.experimental import pallas as pl
from jax.experimental.pallas import tpu as pltpu
from jax.sharding import PartitionSpec as P

STEP_SIZE = 0.5
PENALTY = 0.01
LEVELS = 32767.0
AXIS = "rows"


def soften(values, level):
    return values - jnp.clip(values, -level, level)


def halves(values):
    high = values.astype(jnp.bfloat16)
    low = (values - high.astype(jnp.float32)).astype(jnp.bfloat16)
    return jnp.concatenate([high, low], axis=1)


def times(left, right):
    return lax.dot_general(
        halves(left),
        jnp.concatenate([right, right], axis=0),
        (((1,), (0,)), ((), ())),
        preferred_element_type=jnp.float32,
    )


def times_turned(left, right):
    return lax.dot_general(
        halves(left),
        jnp.concatenate([right, right], axis=1),
        (((1,), (1,)), ((), ())),
        preferred_element_type=jnp.float32,
    )


def peer_of(me, step, n):
    if n & (n - 1):
        return (me + step) % n
    total = 0
    bit = 1
    while bit < n:
        total = total + bit * (((me // bit) % 2 + (step // bit) % 2) % 2)
        bit *= 2
    return total


def kernel(
    n,
    pattern,
    pattern_rows,
    counts,
    samples,
    diag_hbm,
    off_hbm,
    term,
    diag_out,
    off_out,
    objective,
    diag,
    off,
    x_send,
    x_recv,
    parts,
    runs,
    q_send,
    q_recv,
    aux_send,
    aux_recv,
    last,
    logs,
    table_rows,
    table_smem,
    load_sems,
    out_sems,
    x_send_sems,
    x_recv_sems,
    q_send_sems,
    q_recv_sems,
    aux_send_sems,
    aux_recv_sems,
):
    me = lax.axis_index(AXIS)
    rows, edge = diag.shape[0], diag.shape[1]
    entries = off.shape[0]
    columns = samples.shape[2]
    width = 2.0 * columns

    load_diag = pltpu.make_async_copy(diag_hbm, diag, load_sems.at[0])
    load_off = pltpu.make_async_copy(off_hbm, off, load_sems.at[1])
    load_diag.start()
    load_off.start()

    row, col = pattern_rows[0:1, :], pattern_rows[1:2, :]
    blocks = rows * n
    forth, back, top = row * blocks + col, col * blocks + row, blocks * blocks
    ids = lax.broadcasted_iota(jnp.int32, (1, entries), 1)
    low = lax.broadcasted_iota(jnp.int32, (n, entries), 0) * rows
    linked = (col >= low) & (col < low + rows)
    lane = lax.broadcasted_iota(jnp.int32, table_rows.shape, 1)
    found = jnp.zeros(table_rows.shape, jnp.int32)
    for which, key in enumerate((forth, top - forth, back, top - back)):
        least = jnp.min(
            jnp.where(linked, key * entries + ids, (top + 1) * entries),
            axis=1,
            keepdims=True,
        )
        found = jnp.where(lane == which, least, found)
    table_rows[...] = found
    load_table = pltpu.make_async_copy(table_rows, table_smem, load_sems.at[2])
    load_table.start()

    def find(which, peer):
        return table_smem[peer, which] % entries

    barrier = pltpu.get_barrier_semaphore()

    def greet(i, carry):
        pl.semaphore_signal(
            barrier,
            inc=1,
            device_id={AXIS: peer_of(me, n - 1 - i, n)},
            device_id_type=pl.DeviceIdType.MESH,
        )
        return carry

    lax.fori_loop(0, n - 1, greet, 0)

    def remote(source, target, send_sems, recv_sems, peer, mine):
        return pltpu.make_async_remote_copy(
            src_ref=source.at[peer],
            dst_ref=target.at[mine],
            send_sem=send_sems.at[peer],
            recv_sem=recv_sems.at[mine],
            device_id={AXIS: peer},
            device_id_type=pl.DeviceIdType.MESH,
        )

    x_copy = functools.partial(remote, x_send, x_recv, x_send_sems, x_recv_sems)
    q_copy = functools.partial(remote, q_send, q_recv, q_send_sems, q_recv_sems)
    aux_copy = functools.partial(
        remote, aux_send, aux_recv, aux_send_sems, aux_recv_sems
    )

    load_table.wait()
    pl.semaphore_wait(barrier, n - 1)

    def send_samples(i, carry):
        peer = peer_of(me, n - 1 - i, n)
        for slot in range(2):
            entry = find(slot, peer)
            x_send[peer, slot] = samples[pattern[0, entry] % rows]
        x_copy(peer, me).start()
        return carry

    lax.fori_loop(0, n - 1, send_samples, 0)

    eye = lax.broadcasted_iota(jnp.int32, (edge, edge), 0) == lax.broadcasted_iota(
        jnp.int32, (edge, edge), 1
    )
    identity = eye.astype(jnp.float32)

    total = jnp.int32(0)
    for r in range(rows):
        count = counts[r]
        total = total + count
        last[r] = jnp.where(count > 0, rows + total - 1, r)

    load_diag.wait()

    logs[...] = jnp.zeros_like(logs)

    def own_products(r, carry):
        block = diag[r]
        runs[r] = times(block, samples[r])
        logs[...] += jnp.log(jnp.sum(block * identity, axis=0, keepdims=True))
        return carry

    lax.fori_loop(0, rows, own_products, 0)
    load_off.wait()

    def take_samples(i, carry):
        peer = peer_of(me, n - 1 - i, n)
        x_copy(peer, peer).wait_recv()
        for slot in range(2):
            entry = find(2 + slot, peer)
            parts[peer, slot] = times(off[entry], x_recv[peer, slot])
        return carry

    lax.fori_loop(0, n - 1, take_samples, 0)

    def place(entry):
        owner = pattern[1, entry] // rows
        return owner, jnp.where(find(3, owner) == entry, 1, 0)

    def accumulate(entry, carry):
        row = pattern[0, entry] % rows
        before = pattern[0, jnp.maximum(entry - 1, 0)] % rows
        fresh = (entry == 0) | (row != before)
        base = jnp.where(fresh, row, rows + entry - 1)
        owner, slot = place(entry)
        part = parts[owner, slot]
        runs[rows + entry] = runs[base] + jnp.where(entry < total, part, 0.0)
        return carry

    lax.fori_loop(0, entries, accumulate, 0)

    squares = jnp.zeros((1, columns), jnp.float32)
    for r in range(rows):
        values = runs[last[r]]
        squares = squares + jnp.sum(values * values, axis=0, keepdims=True)
    lanes = -logs[...]
    for start in range(0, columns, edge):
        lanes = lanes + squares[:, start : start + edge] / width
    aux_recv[me, 2:3, :] = lanes

    def send_products(i, carry):
        peer = peer_of(me, n - 1 - i, n)
        for slot in range(2):
            entry = find(slot, peer)
            values = runs[last[pattern[0, entry] % rows]]
            other = jnp.where(find(3, peer) == entry, 1, 0)
            product = times_turned(values, x_recv[peer, other])
            parts[peer, slot, :, :edge] = product
            largest = jnp.maximum(
                jnp.max(jnp.abs(product), axis=0, keepdims=True), 1e-30
            )
            coded = jnp.round(product * (LEVELS / largest))
            q_send[peer, slot] = coded.astype(jnp.int32).astype(jnp.int16)
            aux_send[peer, slot : slot + 1, :] = largest / LEVELS
        aux_send[peer, 2:3, :] = lanes
        aux_copy(peer, me).start()
        q_copy(peer, me).start()
        return carry

    lax.fori_loop(0, n - 1, send_products, 0)

    def finish_diag(r, carry):
        product = times_turned(runs[last[r]], samples[r])
        slope = (product + product.T) / width + identity * term[pl.ds(r, 1), :]
        moved = diag[r] - STEP_SIZE * slope
        diag_out[r] = jnp.where(eye, moved, soften(moved, STEP_SIZE * PENALTY))
        return carry

    lax.fori_loop(0, rows, finish_diag, 0)

    def take_products(i, carry):
        peer = peer_of(me, n - 1 - i, n)
        aux_copy(peer, peer).wait_recv()
        q_copy(peer, peer).wait_recv()
        for slot in range(2):
            entry = find(2 + slot, peer)
            sent = jnp.where(find(1, peer) == entry, 1, 0)
            product = parts[peer, sent][:, :edge]
            scale = aux_recv[peer, slot : slot + 1, :]
            coded = q_recv[peer, slot].astype(jnp.int32).astype(jnp.float32)
            slope = (product + (coded * scale).T) / width
            parts[peer, slot, :, edge : 2 * edge] = soften(
                off[entry] - STEP_SIZE * slope, STEP_SIZE * PENALTY
            )
        return carry

    lax.fori_loop(0, n - 1, take_products, 0)

    def store_copy(entry):
        return pltpu.make_async_copy(
            runs.at[rows + entry, :, pl.ds(0, edge)],
            off_out.at[entry],
            out_sems.at[entry],
        )

    def store_off(entry, carry):
        owner, slot = place(entry)
        values = parts[owner, slot][:, edge : 2 * edge]
        runs[rows + entry, :, :edge] = jnp.where(entry < total, values, 0.0)
        store_copy(entry).start()
        return carry

    lax.fori_loop(0, entries, store_off, 0)

    def add_lanes(d, carry):
        return carry + aux_recv[d, 2:3, :]

    lanes = lax.fori_loop(0, n, add_lanes, jnp.zeros((1, edge), jnp.float32))
    objective[...] = jnp.broadcast_to(
        jnp.sum(lanes, axis=1, keepdims=True) / (rows * n * edge), objective.shape
    )

    def drain(i, carry):
        peer = peer_of(me, n - 1 - i, n)
        x_copy(peer, me).wait_send()
        q_copy(peer, me).wait_send()
        aux_copy(peer, me).wait_send()
        return carry

    lax.fori_loop(0, n - 1, drain, 0)

    def drain_out(entry, carry):
        store_copy(entry).wait()
        return carry

    lax.fori_loop(0, entries, drain_out, 0)


def shards(samples, omega_diag, omega_off, pattern, block_count, diag_term):
    n = lax.axis_size(AXIS)
    rows, edge = omega_diag.shape[0], omega_diag.shape[1]
    columns = samples.shape[1]
    entries = omega_off.shape[0]
    f32, bf16, i16 = jnp.float32, jnp.bfloat16, jnp.int16
    smem = pl.BlockSpec(memory_space=pltpu.SMEM)
    vmem = pl.BlockSpec(memory_space=pltpu.VMEM)
    hbm = pl.BlockSpec(memory_space=pl.ANY)
    dma = pltpu.SemaphoreType.DMA
    held = n * 2 * edge * (columns * 8 + edge * 4) + (
        (rows + entries) * edge * columns + entries * edge * edge
    ) * 4
    held = held + rows * edge * (edge * 8 + columns * 2)
    diag_next, off_next, objective = pl.pallas_call(
        functools.partial(kernel, n),
        out_shape=(
            jax.ShapeDtypeStruct(omega_diag.shape, f32),
            jax.ShapeDtypeStruct(omega_off.shape, f32),
            jax.ShapeDtypeStruct((1, edge), f32),
        ),
        in_specs=[smem, vmem, smem, vmem, hbm, hbm, vmem],
        out_specs=(vmem, hbm, vmem),
        scratch_shapes=[
            pltpu.VMEM(omega_diag.shape, f32),
            pltpu.VMEM(omega_off.shape, f32),
            pltpu.VMEM((n, 2, edge, columns), bf16),
            pltpu.VMEM((n, 2, edge, columns), bf16),
            pltpu.VMEM((n, 2, edge, columns), f32),
            pltpu.VMEM((rows + entries, edge, columns), f32),
            pltpu.VMEM((n, 2, edge, edge), i16),
            pltpu.VMEM((n, 2, edge, edge), i16),
            pltpu.VMEM((n, 8, edge), f32),
            pltpu.VMEM((n, 8, edge), f32),
            pltpu.SMEM((rows,), jnp.int32),
            pltpu.VMEM((1, edge), f32),
            pltpu.VMEM((n, 128), jnp.int32),
            pltpu.SMEM((n, 128), jnp.int32),
            dma((3,)),
            dma((entries,)),
        ]
        + [dma((n,))] * 6,
        compiler_params=pltpu.CompilerParams(
            collective_id=0,
            has_side_effects=True,
            vmem_limit_bytes=min(held + (4 << 20), 60 << 20),
        ),
    )(
        pattern.T,
        pattern.T,
        block_count,
        samples.reshape(rows, edge, columns),
        omega_diag,
        omega_off,
        diag_term.reshape(rows, edge),
    )
    return diag_next, off_next, objective[0, :1]


def solution(mesh):
    return jax.shard_map(
        shards,
        mesh=mesh,
        in_specs=(
            P(("groups", "rows"), None),
            P(("groups", "rows"), None, None),
            P(("groups", "rows"), None, None),
            P(("groups", "rows"), None),
            P(("groups", "rows")),
            P(("groups", "rows")),
        ),
        out_specs=(
            P(("groups", "rows"), None, None),
            P(("groups", "rows"), None, None),
            P("groups"),
        ),
        check_vma=False,
    )
```

```python
import functools

import jax
import jax.numpy as jnp
from jax import lax
from jax.experimental import pallas as pl
from jax.experimental.pallas import tpu as pltpu
from jax.sharding import PartitionSpec as P

STEP_SIZE = 0.5
PENALTY = 0.01
LEVELS = 32767.0
AXIS = "rows"


def soften(values, level):
    return values - jnp.clip(values, -level, level)


def halves(values):
    high = values.astype(jnp.bfloat16)
    low = (values - high.astype(jnp.float32)).astype(jnp.bfloat16)
    return jnp.concatenate([high, low], axis=1)


def times(left, right):
    return lax.dot_general(
        halves(left),
        jnp.concatenate([right, right], axis=0),
        (((1,), (0,)), ((), ())),
        preferred_element_type=jnp.float32,
    )


def times_turned(left, right):
    return lax.dot_general(
        halves(left),
        jnp.concatenate([right, right], axis=1),
        (((1,), (1,)), ((), ())),
        preferred_element_type=jnp.float32,
    )


def peer_of(me, step, n):
    if n & (n - 1):
        return (me + step) % n
    total = 0
    bit = 1
    while bit < n:
        total = total + bit * (((me // bit) % 2 + (step // bit) % 2) % 2)
        bit *= 2
    return total


def kernel(
    n,
    pattern_hbm,
    counts_hbm,
    samples_hbm,
    diag_hbm,
    off_hbm,
    term_hbm,
    diag_out,
    off_out,
    objective,
    diag,
    off,
    x_send,
    x_recv,
    parts,
    runs,
    q_send,
    q_recv,
    aux_send,
    aux_recv,
    last,
    logs,
    table_rows,
    table_smem,
    pattern,
    pattern_rows,
    counts,
    samples,
    term,
    load_sems,
    out_sems,
    x_send_sems,
    x_recv_sems,
    q_send_sems,
    q_recv_sems,
    aux_send_sems,
    aux_recv_sems,
):
    me = lax.axis_index(AXIS)
    rows, edge = diag.shape[0], diag.shape[1]
    entries = off.shape[0]
    columns = samples.shape[2]
    width = 2.0 * columns

    def load(source, target, which):
        copy = pltpu.make_async_copy(source, target, load_sems.at[which])
        copy.start()
        return copy

    load_pattern_rows = load(pattern_hbm, pattern_rows, 3)
    load_pattern = load(pattern_hbm, pattern, 4)
    load_samples = load(samples_hbm, samples, 5)
    load_counts = load(counts_hbm, counts, 6)
    load_term = load(term_hbm, term, 7)
    load_diag = pltpu.make_async_copy(diag_hbm, diag, load_sems.at[0])
    load_off = pltpu.make_async_copy(off_hbm, off, load_sems.at[1])
    load_diag.start()
    load_off.start()

    barrier = pltpu.get_barrier_semaphore()

    def greet(i, carry):
        pl.semaphore_signal(
            barrier,
            inc=1,
            device_id={AXIS: peer_of(me, n - 1 - i, n)},
            device_id_type=pl.DeviceIdType.MESH,
        )
        return carry

    lax.fori_loop(0, n - 1, greet, 0)

    load_pattern_rows.wait()
    row, col = pattern_rows[0:1, :], pattern_rows[1:2, :]
    blocks = rows * n
    forth, back, top = row * blocks + col, col * blocks + row, blocks * blocks
    ids = lax.broadcasted_iota(jnp.int32, (1, entries), 1)
    low = lax.broadcasted_iota(jnp.int32, (n, entries), 0) * rows
    linked = (col >= low) & (col < low + rows)
    lane = lax.broadcasted_iota(jnp.int32, table_rows.shape, 1)
    found = jnp.zeros(table_rows.shape, jnp.int32)
    for which, key in enumerate((forth, top - forth, back, top - back)):
        least = jnp.min(
            jnp.where(linked, key * entries + ids, (top + 1) * entries),
            axis=1,
            keepdims=True,
        )
        found = jnp.where(lane == which, least, found)
    table_rows[...] = found
    load_table = pltpu.make_async_copy(table_rows, table_smem, load_sems.at[2])
    load_table.start()

    def find(which, peer):
        return table_smem[peer, which] % entries

    def remote(source, target, send_sems, recv_sems, peer, mine):
        return pltpu.make_async_remote_copy(
            src_ref=source.at[peer],
            dst_ref=target.at[mine],
            send_sem=send_sems.at[peer],
            recv_sem=recv_sems.at[mine],
            device_id={AXIS: peer},
            device_id_type=pl.DeviceIdType.MESH,
        )

    x_copy = functools.partial(remote, x_send, x_recv, x_send_sems, x_recv_sems)
    q_copy = functools.partial(remote, q_send, q_recv, q_send_sems, q_recv_sems)
    aux_copy = functools.partial(
        remote, aux_send, aux_recv, aux_send_sems, aux_recv_sems
    )

    load_pattern.wait()
    load_samples.wait()
    load_table.wait()
    pl.semaphore_wait(barrier, n - 1)

    def send_samples(i, carry):
        peer = peer_of(me, n - 1 - i, n)
        for slot in range(2):
            entry = find(slot, peer)
            x_send[peer, slot] = samples[pattern[0, entry] % rows]
        x_copy(peer, me).start()
        return carry

    lax.fori_loop(0, n - 1, send_samples, 0)

    eye = lax.broadcasted_iota(jnp.int32, (edge, edge), 0) == lax.broadcasted_iota(
        jnp.int32, (edge, edge), 1
    )
    identity = eye.astype(jnp.float32)

    load_counts.wait()
    total = jnp.int32(0)
    for r in range(rows):
        count = counts[r]
        total = total + count
        last[r] = jnp.where(count > 0, rows + total - 1, r)

    load_diag.wait()

    logs[...] = jnp.zeros_like(logs)

    def own_products(r, carry):
        block = diag[r]
        runs[r] = times(block, samples[r])
        logs[...] += jnp.log(jnp.sum(block * identity, axis=0, keepdims=True))
        return carry

    lax.fori_loop(0, rows, own_products, 0)
    load_off.wait()

    def take_samples(i, carry):
        peer = peer_of(me, i + 1, n)
        x_copy(peer, peer).wait_recv()
        for slot in range(2):
            entry = find(2 + slot, peer)
            parts[peer, slot] = times(off[entry], x_recv[peer, slot])
        return carry

    lax.fori_loop(0, n - 1, take_samples, 0)

    def place(entry):
        owner = pattern[1, entry] // rows
        return owner, jnp.where(find(3, owner) == entry, 1, 0)

    def accumulate(entry, carry):
        row = pattern[0, entry] % rows
        before = pattern[0, jnp.maximum(entry - 1, 0)] % rows
        fresh = (entry == 0) | (row != before)
        base = jnp.where(fresh, row, rows + entry - 1)
        owner, slot = place(entry)
        part = parts[owner, slot]
        runs[rows + entry] = runs[base] + jnp.where(entry < total, part, 0.0)
        return carry

    lax.fori_loop(0, entries, accumulate, 0)

    squares = jnp.zeros((1, columns), jnp.float32)
    for r in range(rows):
        values = runs[last[r]]
        squares = squares + jnp.sum(values * values, axis=0, keepdims=True)
    lanes = -logs[...]
    for start in range(0, columns, edge):
        lanes = lanes + squares[:, start : start + edge] / width
    aux_recv[me, 2:3, :] = lanes

    def send_products(i, carry):
        peer = peer_of(me, n - 1 - i, n)
        for slot in range(2):
            entry = find(slot, peer)
            values = runs[last[pattern[0, entry] % rows]]
            other = jnp.where(find(3, peer) == entry, 1, 0)
            product = times_turned(values, x_recv[peer, other])
            parts[peer, slot, :, :edge] = product
            largest = jnp.maximum(
                jnp.max(jnp.abs(product), axis=0, keepdims=True), 1e-30
            )
            coded = jnp.round(product * (LEVELS / largest))
            q_send[peer, slot] = coded.astype(jnp.int32).astype(jnp.int16)
            aux_send[peer, slot : slot + 1, :] = largest / LEVELS
        aux_send[peer, 2:3, :] = lanes
        aux_copy(peer, me).start()
        q_copy(peer, me).start()
        return carry

    lax.fori_loop(0, n - 1, send_products, 0)

    def finish_diag(r, carry):
        product = times_turned(runs[last[r]], samples[r])
        slope = (product + product.T) / width + identity * term[pl.ds(r, 1), :]
        moved = diag[r] - STEP_SIZE * slope
        diag_out[r] = jnp.where(eye, moved, soften(moved, STEP_SIZE * PENALTY))
        return carry

    load_term.wait()
    lax.fori_loop(0, rows, finish_diag, 0)

    def take_products(i, carry):
        peer = peer_of(me, i + 1, n)
        aux_copy(peer, peer).wait_recv()
        q_copy(peer, peer).wait_recv()
        for slot in range(2):
            entry = find(2 + slot, peer)
            sent = jnp.where(find(1, peer) == entry, 1, 0)
            product = parts[peer, sent][:, :edge]
            scale = aux_recv[peer, slot : slot + 1, :]
            coded = q_recv[peer, slot].astype(jnp.int32).astype(jnp.float32)
            slope = (product + (coded * scale).T) / width
            parts[peer, slot, :, edge : 2 * edge] = soften(
                off[entry] - STEP_SIZE * slope, STEP_SIZE * PENALTY
            )
        return carry

    lax.fori_loop(0, n - 1, take_products, 0)

    def store_copy(entry):
        return pltpu.make_async_copy(
            runs.at[rows + entry, :, pl.ds(0, edge)],
            off_out.at[entry],
            out_sems.at[entry],
        )

    def store_off(entry, carry):
        owner, slot = place(entry)
        values = parts[owner, slot][:, edge : 2 * edge]
        runs[rows + entry, :, :edge] = jnp.where(entry < total, values, 0.0)
        store_copy(entry).start()
        return carry

    lax.fori_loop(0, entries, store_off, 0)

    def add_lanes(d, carry):
        return carry + aux_recv[d, 2:3, :]

    lanes = lax.fori_loop(0, n, add_lanes, jnp.zeros((1, edge), jnp.float32))
    objective[...] = jnp.broadcast_to(
        jnp.sum(lanes, axis=1, keepdims=True) / (rows * n * edge), objective.shape
    )

    def drain(i, carry):
        peer = peer_of(me, n - 1 - i, n)
        x_copy(peer, me).wait_send()
        q_copy(peer, me).wait_send()
        aux_copy(peer, me).wait_send()
        return carry

    lax.fori_loop(0, n - 1, drain, 0)

    def drain_out(entry, carry):
        store_copy(entry).wait()
        return carry

    lax.fori_loop(0, entries, drain_out, 0)


def shards(samples, omega_diag, omega_off, pattern, block_count, diag_term):
    n = lax.axis_size(AXIS)
    rows, edge = omega_diag.shape[0], omega_diag.shape[1]
    columns = samples.shape[1]
    entries = omega_off.shape[0]
    f32, bf16, i16 = jnp.float32, jnp.bfloat16, jnp.int16
    vmem = pl.BlockSpec(memory_space=pltpu.VMEM)
    hbm = pl.BlockSpec(memory_space=pl.ANY)
    dma = pltpu.SemaphoreType.DMA
    held = n * 2 * edge * (columns * 8 + edge * 4) + (
        (rows + entries) * edge * columns + entries * edge * edge
    ) * 4
    held = held + rows * edge * (edge * 8 + columns * 2)
    diag_next, off_next, objective = pl.pallas_call(
        functools.partial(kernel, n),
        out_shape=(
            jax.ShapeDtypeStruct(omega_diag.shape, f32),
            jax.ShapeDtypeStruct(omega_off.shape, f32),
            jax.ShapeDtypeStruct((1, edge), f32),
        ),
        in_specs=[pl.BlockSpec(memory_space=pltpu.HBM)] * 6,
        out_specs=(vmem, hbm, vmem),
        scratch_shapes=[
            pltpu.VMEM(omega_diag.shape, f32),
            pltpu.VMEM(omega_off.shape, f32),
            pltpu.VMEM((n, 2, edge, columns), bf16),
            pltpu.VMEM((n, 2, edge, columns), bf16),
            pltpu.VMEM((n, 2, edge, columns), f32),
            pltpu.VMEM((rows + entries, edge, columns), f32),
            pltpu.VMEM((n, 2, edge, edge), i16),
            pltpu.VMEM((n, 2, edge, edge), i16),
            pltpu.VMEM((n, 8, edge), f32),
            pltpu.VMEM((n, 8, edge), f32),
            pltpu.SMEM((rows,), jnp.int32),
            pltpu.VMEM((1, edge), f32),
            pltpu.VMEM((n, 128), jnp.int32),
            pltpu.SMEM((n, 128), jnp.int32),
            pltpu.SMEM((2, entries), jnp.int32),
            pltpu.VMEM((2, entries), jnp.int32),
            pltpu.SMEM((rows,), jnp.int32),
            pltpu.VMEM((rows, edge, columns), bf16),
            pltpu.VMEM((rows, edge), f32),
            dma((8,)),
            dma((entries,)),
        ]
        + [dma((n,))] * 6,
        compiler_params=pltpu.CompilerParams(
            collective_id=0,
            has_side_effects=True,
            vmem_limit_bytes=min(held + (4 << 20), 60 << 20),
        ),
    )(
        *(
            pltpu.with_memory_space_constraint(value, pltpu.HBM)
            for value in (
                pattern.T,
                block_count,
                samples.reshape(rows, edge, columns),
                omega_diag,
                omega_off,
                diag_term.reshape(rows, edge),
            )
        )
    )
    return diag_next, off_next, objective[0, :1]


def solution(mesh):
    return jax.shard_map(
        shards,
        mesh=mesh,
        in_specs=(
            P(("groups", "rows"), None),
            P(("groups", "rows"), None, None),
            P(("groups", "rows"), None, None),
            P(("groups", "rows"), None),
            P(("groups", "rows")),
            P(("groups", "rows")),
        ),
        out_specs=(
            P(("groups", "rows"), None, None),
            P(("groups", "rows"), None, None),
            P("groups"),
        ),
        check_vma=False,
    )
```

```python
import functools

import jax
import jax.numpy as jnp
from jax import lax
from jax.experimental import pallas as pl
from jax.experimental.pallas import tpu as pltpu
from jax.sharding import PartitionSpec as P

STEP_SIZE = 0.5
PENALTY = 0.01
LEVELS = 32767.0
AXIS = "rows"


def soften(values, level):
    return values - jnp.clip(values, -level, level)


def halves(values):
    high = values.astype(jnp.bfloat16)
    low = (values - high.astype(jnp.float32)).astype(jnp.bfloat16)
    return jnp.concatenate([high, low], axis=1)


def times(left, right):
    return lax.dot_general(
        halves(left),
        jnp.concatenate([right, right], axis=0),
        (((1,), (0,)), ((), ())),
        preferred_element_type=jnp.float32,
    )


def times_turned(left, right):
    return lax.dot_general(
        halves(left),
        jnp.concatenate([right, right], axis=1),
        (((1,), (1,)), ((), ())),
        preferred_element_type=jnp.float32,
    )


def peer_of(me, step, n):
    if n & (n - 1):
        return (me + step) % n
    total = 0
    bit = 1
    while bit < n:
        total = total + bit * (((me // bit) % 2 + (step // bit) % 2) % 2)
        bit *= 2
    return total


def spread(i, n):
    half, odd = (i + 1) // 2, i % 2
    return odd * half + (1 - odd) * (n - 1 - half)


def kernel(
    n,
    pattern_hbm,
    counts_hbm,
    samples_hbm,
    diag_hbm,
    off_hbm,
    term_hbm,
    diag_out,
    off_out,
    objective,
    diag,
    off,
    x_send,
    x_recv,
    parts,
    runs,
    q_send,
    q_recv,
    aux_send,
    aux_recv,
    last,
    logs,
    table_rows,
    table_smem,
    pattern,
    pattern_rows,
    counts,
    samples,
    term,
    load_sems,
    out_sems,
    x_send_sems,
    x_recv_sems,
    q_send_sems,
    q_recv_sems,
    aux_send_sems,
    aux_recv_sems,
):
    me = lax.axis_index(AXIS)
    rows, edge = diag.shape[0], diag.shape[1]
    entries = off.shape[0]
    columns = samples.shape[2]
    width = 2.0 * columns

    def load(source, target, which):
        copy = pltpu.make_async_copy(source, target, load_sems.at[which])
        copy.start()
        return copy

    load_pattern_rows = load(pattern_hbm, pattern_rows, 3)
    load_pattern = load(pattern_hbm, pattern, 4)
    load_samples = load(samples_hbm, samples, 5)
    load_counts = load(counts_hbm, counts, 6)
    load_term = load(term_hbm, term, 7)
    load_diag = pltpu.make_async_copy(diag_hbm, diag, load_sems.at[0])
    load_off = pltpu.make_async_copy(off_hbm, off, load_sems.at[1])
    load_diag.start()
    load_off.start()

    barrier = pltpu.get_barrier_semaphore()

    def greet(i, carry):
        pl.semaphore_signal(
            barrier,
            inc=1,
            device_id={AXIS: peer_of(me, spread(i, n), n)},
            device_id_type=pl.DeviceIdType.MESH,
        )
        return carry

    lax.fori_loop(0, n - 1, greet, 0)

    load_pattern_rows.wait()
    row, col = pattern_rows[0:1, :], pattern_rows[1:2, :]
    blocks = rows * n
    forth, back, top = row * blocks + col, col * blocks + row, blocks * blocks
    ids = lax.broadcasted_iota(jnp.int32, (1, entries), 1)
    low = lax.broadcasted_iota(jnp.int32, (n, entries), 0) * rows
    linked = (col >= low) & (col < low + rows)
    lane = lax.broadcasted_iota(jnp.int32, table_rows.shape, 1)
    found = jnp.zeros(table_rows.shape, jnp.int32)
    for which, key in enumerate((forth, top - forth, back, top - back)):
        least = jnp.min(
            jnp.where(linked, key * entries + ids, (top + 1) * entries),
            axis=1,
            keepdims=True,
        )
        found = jnp.where(lane == which, least, found)
    table_rows[...] = found
    load_table = pltpu.make_async_copy(table_rows, table_smem, load_sems.at[2])
    load_table.start()

    def find(which, peer):
        return table_smem[peer, which] % entries

    def remote(source, target, send_sems, recv_sems, peer, mine):
        return pltpu.make_async_remote_copy(
            src_ref=source.at[peer],
            dst_ref=target.at[mine],
            send_sem=send_sems.at[peer],
            recv_sem=recv_sems.at[mine],
            device_id={AXIS: peer},
            device_id_type=pl.DeviceIdType.MESH,
        )

    x_copy = functools.partial(remote, x_send, x_recv, x_send_sems, x_recv_sems)
    q_copy = functools.partial(remote, q_send, q_recv, q_send_sems, q_recv_sems)
    aux_copy = functools.partial(
        remote, aux_send, aux_recv, aux_send_sems, aux_recv_sems
    )

    load_pattern.wait()
    load_samples.wait()
    load_table.wait()
    pl.semaphore_wait(barrier, n - 1)

    def send_samples(i, carry):
        peer = peer_of(me, spread(i, n), n)
        for slot in range(2):
            entry = find(slot, peer)
            x_send[peer, slot] = samples[pattern[0, entry] % rows]
        x_copy(peer, me).start()
        return carry

    lax.fori_loop(0, n - 1, send_samples, 0)

    eye = lax.broadcasted_iota(jnp.int32, (edge, edge), 0) == lax.broadcasted_iota(
        jnp.int32, (edge, edge), 1
    )
    identity = eye.astype(jnp.float32)

    load_counts.wait()
    total = jnp.int32(0)
    for r in range(rows):
        count = counts[r]
        total = total + count
        last[r] = jnp.where(count > 0, rows + total - 1, r)

    load_diag.wait()

    logs[...] = jnp.zeros_like(logs)

    def own_products(r, carry):
        block = diag[r]
        runs[r] = times(block, samples[r])
        logs[...] += jnp.log(jnp.sum(block * identity, axis=0, keepdims=True))
        return carry

    lax.fori_loop(0, rows, own_products, 0)
    load_off.wait()

    def take_samples(i, carry):
        peer = peer_of(me, spread(i, n), n)
        x_copy(peer, peer).wait_recv()
        for slot in range(2):
            entry = find(2 + slot, peer)
            parts[peer, slot] = times(off[entry], x_recv[peer, slot])
        return carry

    lax.fori_loop(0, n - 1, take_samples, 0)

    def place(entry):
        owner = pattern[1, entry] // rows
        return owner, jnp.where(find(3, owner) == entry, 1, 0)

    def accumulate(entry, carry):
        row = pattern[0, entry] % rows
        before = pattern[0, jnp.maximum(entry - 1, 0)] % rows
        fresh = (entry == 0) | (row != before)
        base = jnp.where(fresh, row, rows + entry - 1)
        owner, slot = place(entry)
        part = parts[owner, slot]
        runs[rows + entry] = runs[base] + jnp.where(entry < total, part, 0.0)
        return carry

    lax.fori_loop(0, entries, accumulate, 0)

    squares = jnp.zeros((1, columns), jnp.float32)
    for r in range(rows):
        values = runs[last[r]]
        squares = squares + jnp.sum(values * values, axis=0, keepdims=True)
    lanes = -logs[...]
    for start in range(0, columns, edge):
        lanes = lanes + squares[:, start : start + edge] / width
    aux_recv[me, 2:3, :] = lanes

    def send_products(i, carry):
        peer = peer_of(me, spread(i, n), n)
        for slot in range(2):
            entry = find(slot, peer)
            values = runs[last[pattern[0, entry] % rows]]
            other = jnp.where(find(3, peer) == entry, 1, 0)
            product = times_turned(values, x_recv[peer, other])
            parts[peer, slot, :, :edge] = product
            largest = jnp.maximum(
                jnp.max(jnp.abs(product), axis=0, keepdims=True), 1e-30
            )
            coded = jnp.round(product * (LEVELS / largest))
            q_send[peer, slot] = coded.astype(jnp.int32).astype(jnp.int16)
            aux_send[peer, slot : slot + 1, :] = largest / LEVELS
        aux_send[peer, 2:3, :] = lanes
        aux_copy(peer, me).start()
        q_copy(peer, me).start()
        return carry

    lax.fori_loop(0, n - 1, send_products, 0)

    def finish_diag(r, carry):
        product = times_turned(runs[last[r]], samples[r])
        slope = (product + product.T) / width + identity * term[pl.ds(r, 1), :]
        moved = diag[r] - STEP_SIZE * slope
        diag_out[r] = jnp.where(eye, moved, soften(moved, STEP_SIZE * PENALTY))
        return carry

    load_term.wait()
    lax.fori_loop(0, rows, finish_diag, 0)

    def take_products(i, carry):
        peer = peer_of(me, spread(i, n), n)
        aux_copy(peer, peer).wait_recv()
        q_copy(peer, peer).wait_recv()
        for slot in range(2):
            entry = find(2 + slot, peer)
            sent = jnp.where(find(1, peer) == entry, 1, 0)
            product = parts[peer, sent][:, :edge]
            scale = aux_recv[peer, slot : slot + 1, :]
            coded = q_recv[peer, slot].astype(jnp.int32).astype(jnp.float32)
            slope = (product + (coded * scale).T) / width
            parts[peer, slot, :, edge : 2 * edge] = soften(
                off[entry] - STEP_SIZE * slope, STEP_SIZE * PENALTY
            )
        return carry

    lax.fori_loop(0, n - 1, take_products, 0)

    def store_copy(entry):
        return pltpu.make_async_copy(
            runs.at[rows + entry, :, pl.ds(0, edge)],
            off_out.at[entry],
            out_sems.at[entry],
        )

    def store_off(entry, carry):
        owner, slot = place(entry)
        values = parts[owner, slot][:, edge : 2 * edge]
        runs[rows + entry, :, :edge] = jnp.where(entry < total, values, 0.0)
        store_copy(entry).start()
        return carry

    lax.fori_loop(0, entries, store_off, 0)

    def add_lanes(d, carry):
        return carry + aux_recv[d, 2:3, :]

    lanes = lax.fori_loop(0, n, add_lanes, jnp.zeros((1, edge), jnp.float32))
    objective[...] = jnp.broadcast_to(
        jnp.sum(lanes, axis=1, keepdims=True) / (rows * n * edge), objective.shape
    )

    def drain(i, carry):
        peer = peer_of(me, spread(i, n), n)
        x_copy(peer, me).wait_send()
        q_copy(peer, me).wait_send()
        aux_copy(peer, me).wait_send()
        return carry

    lax.fori_loop(0, n - 1, drain, 0)

    def drain_out(entry, carry):
        store_copy(entry).wait()
        return carry

    lax.fori_loop(0, entries, drain_out, 0)


def shards(samples, omega_diag, omega_off, pattern, block_count, diag_term):
    n = lax.axis_size(AXIS)
    rows, edge = omega_diag.shape[0], omega_diag.shape[1]
    columns = samples.shape[1]
    entries = omega_off.shape[0]
    f32, bf16, i16 = jnp.float32, jnp.bfloat16, jnp.int16
    vmem = pl.BlockSpec(memory_space=pltpu.VMEM)
    hbm = pl.BlockSpec(memory_space=pl.ANY)
    dma = pltpu.SemaphoreType.DMA
    held = n * 2 * edge * (columns * 8 + edge * 4) + (
        (rows + entries) * edge * columns + entries * edge * edge
    ) * 4
    held = held + rows * edge * (edge * 8 + columns * 2)
    diag_next, off_next, objective = pl.pallas_call(
        functools.partial(kernel, n),
        out_shape=(
            jax.ShapeDtypeStruct(omega_diag.shape, f32),
            jax.ShapeDtypeStruct(omega_off.shape, f32),
            jax.ShapeDtypeStruct((1, edge), f32),
        ),
        in_specs=[pl.BlockSpec(memory_space=pltpu.HBM)] * 6,
        out_specs=(vmem, hbm, vmem),
        scratch_shapes=[
            pltpu.VMEM(omega_diag.shape, f32),
            pltpu.VMEM(omega_off.shape, f32),
            pltpu.VMEM((n, 2, edge, columns), bf16),
            pltpu.VMEM((n, 2, edge, columns), bf16),
            pltpu.VMEM((n, 2, edge, columns), f32),
            pltpu.VMEM((rows + entries, edge, columns), f32),
            pltpu.VMEM((n, 2, edge, edge), i16),
            pltpu.VMEM((n, 2, edge, edge), i16),
            pltpu.VMEM((n, 8, edge), f32),
            pltpu.VMEM((n, 8, edge), f32),
            pltpu.SMEM((rows,), jnp.int32),
            pltpu.VMEM((1, edge), f32),
            pltpu.VMEM((n, 128), jnp.int32),
            pltpu.SMEM((n, 128), jnp.int32),
            pltpu.SMEM((2, entries), jnp.int32),
            pltpu.VMEM((2, entries), jnp.int32),
            pltpu.SMEM((rows,), jnp.int32),
            pltpu.VMEM((rows, edge, columns), bf16),
            pltpu.VMEM((rows, edge), f32),
            dma((8,)),
            dma((entries,)),
        ]
        + [dma((n,))] * 6,
        compiler_params=pltpu.CompilerParams(
            collective_id=0,
            has_side_effects=True,
            vmem_limit_bytes=min(held + (4 << 20), 60 << 20),
        ),
    )(
        *(
            pltpu.with_memory_space_constraint(value, pltpu.HBM)
            for value in (
                pattern.T,
                block_count,
                samples.reshape(rows, edge, columns),
                omega_diag,
                omega_off,
                diag_term.reshape(rows, edge),
            )
        )
    )
    return diag_next, off_next, objective[0, :1]


def solution(mesh):
    return jax.shard_map(
        shards,
        mesh=mesh,
        in_specs=(
            P(("groups", "rows"), None),
            P(("groups", "rows"), None, None),
            P(("groups", "rows"), None, None),
            P(("groups", "rows"), None),
            P(("groups", "rows")),
            P(("groups", "rows")),
        ),
        out_specs=(
            P(("groups", "rows"), None, None),
            P(("groups", "rows"), None, None),
            P("groups"),
        ),
        check_vma=False,
    )
```

```python
import functools

import jax
import jax.numpy as jnp
from jax import lax
from jax.experimental import pallas as pl
from jax.experimental.pallas import tpu as pltpu
from jax.sharding import PartitionSpec as P

STEP_SIZE = 0.5
PENALTY = 0.01
LEVELS = 32767.0
AXIS = "rows"


def soften(values, level):
    return values - jnp.clip(values, -level, level)


def halves(values):
    high = values.astype(jnp.bfloat16)
    low = (values - high.astype(jnp.float32)).astype(jnp.bfloat16)
    return jnp.concatenate([high, low], axis=1)


def times(left, right):
    return lax.dot_general(
        halves(left),
        jnp.concatenate([right, right], axis=0),
        (((1,), (0,)), ((), ())),
        preferred_element_type=jnp.float32,
    )


def times_turned(left, right):
    return lax.dot_general(
        halves(left),
        jnp.concatenate([right, right], axis=1),
        (((1,), (1,)), ((), ())),
        preferred_element_type=jnp.float32,
    )


def peer_of(me, step, n):
    if n & (n - 1):
        return (me + step) % n
    total = 0
    bit = 1
    while bit < n:
        total = total + bit * (((me // bit) % 2 + (step // bit) % 2) % 2)
        bit *= 2
    return total


def spread(i, n):
    half, odd = (i + 1) // 2, i % 2
    return odd * half + (1 - odd) * (n - 1 - half)


def kernel(
    n,
    pattern_hbm,
    counts_hbm,
    samples_hbm,
    diag_hbm,
    off_hbm,
    term_hbm,
    diag_out,
    off_out,
    objective,
    diag,
    off,
    x_send,
    x_recv,
    parts,
    runs,
    q_send,
    q_recv,
    aux_send,
    aux_recv,
    last,
    logs,
    table_rows,
    table_smem,
    pattern,
    pattern_rows,
    counts,
    samples,
    term,
    load_sems,
    out_sems,
    x_send_sems,
    x_recv_sems,
    q_send_sems,
    q_recv_sems,
    aux_send_sems,
    aux_recv_sems,
):
    me = lax.axis_index(AXIS)
    rows, edge = diag.shape[0], diag.shape[1]
    entries = off.shape[0]
    columns = samples.shape[2]
    width = 2.0 * columns

    def load(source, target, which):
        copy = pltpu.make_async_copy(source, target, load_sems.at[which])
        copy.start()
        return copy

    load_pattern_rows = load(pattern_hbm, pattern_rows, 3)
    load_pattern = load(pattern_hbm, pattern, 4)
    load_samples = load(samples_hbm, samples, 5)
    load_counts = load(counts_hbm, counts, 6)
    load_term = load(term_hbm, term, 7)
    load_diag = pltpu.make_async_copy(diag_hbm, diag, load_sems.at[0])
    load_off = pltpu.make_async_copy(off_hbm, off, load_sems.at[1])
    load_diag.start()
    load_off.start()

    barrier = pltpu.get_barrier_semaphore()

    def greet(i, carry):
        pl.semaphore_signal(
            barrier,
            inc=1,
            device_id={AXIS: peer_of(me, spread((i + me % 2) % (n - 1), n), n)},
            device_id_type=pl.DeviceIdType.MESH,
        )
        return carry

    lax.fori_loop(0, n - 1, greet, 0)

    load_pattern_rows.wait()
    row, col = pattern_rows[0:1, :], pattern_rows[1:2, :]
    blocks = rows * n
    forth, back, top = row * blocks + col, col * blocks + row, blocks * blocks
    ids = lax.broadcasted_iota(jnp.int32, (1, entries), 1)
    low = lax.broadcasted_iota(jnp.int32, (n, entries), 0) * rows
    linked = (col >= low) & (col < low + rows)
    lane = lax.broadcasted_iota(jnp.int32, table_rows.shape, 1)
    found = jnp.zeros(table_rows.shape, jnp.int32)
    for which, key in enumerate((forth, top - forth, back, top - back)):
        least = jnp.min(
            jnp.where(linked, key * entries + ids, (top + 1) * entries),
            axis=1,
            keepdims=True,
        )
        found = jnp.where(lane == which, least, found)
    table_rows[...] = found
    load_table = pltpu.make_async_copy(table_rows, table_smem, load_sems.at[2])
    load_table.start()

    def find(which, peer):
        return table_smem[peer, which] % entries

    def remote(source, target, send_sems, recv_sems, peer, mine):
        return pltpu.make_async_remote_copy(
            src_ref=source.at[peer],
            dst_ref=target.at[mine],
            send_sem=send_sems.at[peer],
            recv_sem=recv_sems.at[mine],
            device_id={AXIS: peer},
            device_id_type=pl.DeviceIdType.MESH,
        )

    x_copy = functools.partial(remote, x_send, x_recv, x_send_sems, x_recv_sems)
    q_copy = functools.partial(remote, q_send, q_recv, q_send_sems, q_recv_sems)
    aux_copy = functools.partial(
        remote, aux_send, aux_recv, aux_send_sems, aux_recv_sems
    )

    load_pattern.wait()
    load_samples.wait()
    load_table.wait()
    pl.semaphore_wait(barrier, n - 1)

    def send_samples(i, carry):
        peer = peer_of(me, spread((i + me % 2) % (n - 1), n), n)
        for slot in range(2):
            entry = find(slot, peer)
            x_send[peer, slot] = samples[pattern[0, entry] % rows]
        x_copy(peer, me).start()
        return carry

    lax.fori_loop(0, n - 1, send_samples, 0)

    eye = lax.broadcasted_iota(jnp.int32, (edge, edge), 0) == lax.broadcasted_iota(
        jnp.int32, (edge, edge), 1
    )
    identity = eye.astype(jnp.float32)

    load_counts.wait()
    total = jnp.int32(0)
    for r in range(rows):
        count = counts[r]
        total = total + count
        last[r] = jnp.where(count > 0, rows + total - 1, r)

    load_diag.wait()

    logs[...] = jnp.zeros_like(logs)

    def own_products(r, carry):
        block = diag[r]
        runs[r] = times(block, samples[r])
        logs[...] += jnp.log(jnp.sum(block * identity, axis=0, keepdims=True))
        return carry

    lax.fori_loop(0, rows, own_products, 0)
    load_off.wait()

    def take_samples(i, carry):
        peer = peer_of(me, spread((i + me % 2) % (n - 1), n), n)
        x_copy(peer, peer).wait_recv()
        for slot in range(2):
            entry = find(2 + slot, peer)
            parts[peer, slot] = times(off[entry], x_recv[peer, slot])
        return carry

    lax.fori_loop(0, n - 1, take_samples, 0)

    def place(entry):
        owner = pattern[1, entry] // rows
        return owner, jnp.where(find(3, owner) == entry, 1, 0)

    def accumulate(entry, carry):
        row = pattern[0, entry] % rows
        before = pattern[0, jnp.maximum(entry - 1, 0)] % rows
        fresh = (entry == 0) | (row != before)
        base = jnp.where(fresh, row, rows + entry - 1)
        owner, slot = place(entry)
        part = parts[owner, slot]
        runs[rows + entry] = runs[base] + jnp.where(entry < total, part, 0.0)
        return carry

    lax.fori_loop(0, entries, accumulate, 0)

    squares = jnp.zeros((1, columns), jnp.float32)
    for r in range(rows):
        values = runs[last[r]]
        squares = squares + jnp.sum(values * values, axis=0, keepdims=True)
    lanes = -logs[...]
    for start in range(0, columns, edge):
        lanes = lanes + squares[:, start : start + edge] / width
    aux_recv[me, 2:3, :] = lanes

    def send_products(i, carry):
        peer = peer_of(me, spread((i + me % 2) % (n - 1), n), n)
        for slot in range(2):
            entry = find(slot, peer)
            values = runs[last[pattern[0, entry] % rows]]
            other = jnp.where(find(3, peer) == entry, 1, 0)
            product = times_turned(values, x_recv[peer, other])
            parts[peer, slot, :, :edge] = product
            largest = jnp.maximum(
                jnp.max(jnp.abs(product), axis=0, keepdims=True), 1e-30
            )
            coded = jnp.round(product * (LEVELS / largest))
            q_send[peer, slot] = coded.astype(jnp.int32).astype(jnp.int16)
            aux_send[peer, slot : slot + 1, :] = largest / LEVELS
        aux_send[peer, 2:3, :] = lanes
        aux_copy(peer, me).start()
        q_copy(peer, me).start()
        return carry

    lax.fori_loop(0, n - 1, send_products, 0)

    def finish_diag(r, carry):
        product = times_turned(runs[last[r]], samples[r])
        slope = (product + product.T) / width + identity * term[pl.ds(r, 1), :]
        moved = diag[r] - STEP_SIZE * slope
        diag_out[r] = jnp.where(eye, moved, soften(moved, STEP_SIZE * PENALTY))
        return carry

    load_term.wait()
    lax.fori_loop(0, rows, finish_diag, 0)

    def take_products(i, carry):
        peer = peer_of(me, spread((i + me % 2) % (n - 1), n), n)
        aux_copy(peer, peer).wait_recv()
        q_copy(peer, peer).wait_recv()
        for slot in range(2):
            entry = find(2 + slot, peer)
            sent = jnp.where(find(1, peer) == entry, 1, 0)
            product = parts[peer, sent][:, :edge]
            scale = aux_recv[peer, slot : slot + 1, :]
            coded = q_recv[peer, slot].astype(jnp.int32).astype(jnp.float32)
            slope = (product + (coded * scale).T) / width
            parts[peer, slot, :, edge : 2 * edge] = soften(
                off[entry] - STEP_SIZE * slope, STEP_SIZE * PENALTY
            )
        return carry

    lax.fori_loop(0, n - 1, take_products, 0)

    def store_copy(entry):
        return pltpu.make_async_copy(
            runs.at[rows + entry, :, pl.ds(0, edge)],
            off_out.at[entry],
            out_sems.at[entry],
        )

    def store_off(entry, carry):
        owner, slot = place(entry)
        values = parts[owner, slot][:, edge : 2 * edge]
        runs[rows + entry, :, :edge] = jnp.where(entry < total, values, 0.0)
        store_copy(entry).start()
        return carry

    lax.fori_loop(0, entries, store_off, 0)

    def add_lanes(d, carry):
        return carry + aux_recv[d, 2:3, :]

    lanes = lax.fori_loop(0, n, add_lanes, jnp.zeros((1, edge), jnp.float32))
    objective[...] = jnp.broadcast_to(
        jnp.sum(lanes, axis=1, keepdims=True) / (rows * n * edge), objective.shape
    )

    def drain(i, carry):
        peer = peer_of(me, spread((i + me % 2) % (n - 1), n), n)
        x_copy(peer, me).wait_send()
        q_copy(peer, me).wait_send()
        aux_copy(peer, me).wait_send()
        return carry

    lax.fori_loop(0, n - 1, drain, 0)

    def drain_out(entry, carry):
        store_copy(entry).wait()
        return carry

    lax.fori_loop(0, entries, drain_out, 0)


def shards(samples, omega_diag, omega_off, pattern, block_count, diag_term):
    n = lax.axis_size(AXIS)
    rows, edge = omega_diag.shape[0], omega_diag.shape[1]
    columns = samples.shape[1]
    entries = omega_off.shape[0]
    f32, bf16, i16 = jnp.float32, jnp.bfloat16, jnp.int16
    vmem = pl.BlockSpec(memory_space=pltpu.VMEM)
    hbm = pl.BlockSpec(memory_space=pl.ANY)
    dma = pltpu.SemaphoreType.DMA
    held = n * 2 * edge * (columns * 8 + edge * 4) + (
        (rows + entries) * edge * columns + entries * edge * edge
    ) * 4
    held = held + rows * edge * (edge * 8 + columns * 2)
    diag_next, off_next, objective = pl.pallas_call(
        functools.partial(kernel, n),
        out_shape=(
            jax.ShapeDtypeStruct(omega_diag.shape, f32),
            jax.ShapeDtypeStruct(omega_off.shape, f32),
            jax.ShapeDtypeStruct((1, edge), f32),
        ),
        in_specs=[pl.BlockSpec(memory_space=pltpu.HBM)] * 6,
        out_specs=(vmem, hbm, vmem),
        scratch_shapes=[
            pltpu.VMEM(omega_diag.shape, f32),
            pltpu.VMEM(omega_off.shape, f32),
            pltpu.VMEM((n, 2, edge, columns), bf16),
            pltpu.VMEM((n, 2, edge, columns), bf16),
            pltpu.VMEM((n, 2, edge, columns), f32),
            pltpu.VMEM((rows + entries, edge, columns), f32),
            pltpu.VMEM((n, 2, edge, edge), i16),
            pltpu.VMEM((n, 2, edge, edge), i16),
            pltpu.VMEM((n, 8, edge), f32),
            pltpu.VMEM((n, 8, edge), f32),
            pltpu.SMEM((rows,), jnp.int32),
            pltpu.VMEM((1, edge), f32),
            pltpu.VMEM((n, 128), jnp.int32),
            pltpu.SMEM((n, 128), jnp.int32),
            pltpu.SMEM((2, entries), jnp.int32),
            pltpu.VMEM((2, entries), jnp.int32),
            pltpu.SMEM((rows,), jnp.int32),
            pltpu.VMEM((rows, edge, columns), bf16),
            pltpu.VMEM((rows, edge), f32),
            dma((8,)),
            dma((entries,)),
        ]
        + [dma((n,))] * 6,
        compiler_params=pltpu.CompilerParams(
            collective_id=0,
            has_side_effects=True,
            vmem_limit_bytes=min(held + (4 << 20), 60 << 20),
        ),
    )(
        *(
            pltpu.with_memory_space_constraint(value, pltpu.HBM)
            for value in (
                pattern.T,
                block_count,
                samples.reshape(rows, edge, columns),
                omega_diag,
                omega_off,
                diag_term.reshape(rows, edge),
            )
        )
    )
    return diag_next, off_next, objective[0, :1]


def solution(mesh):
    return jax.shard_map(
        shards,
        mesh=mesh,
        in_specs=(
            P(("groups", "rows"), None),
            P(("groups", "rows"), None, None),
            P(("groups", "rows"), None, None),
            P(("groups", "rows"), None),
            P(("groups", "rows")),
            P(("groups", "rows")),
        ),
        out_specs=(
            P(("groups", "rows"), None, None),
            P(("groups", "rows"), None, None),
            P("groups"),
        ),
        check_vma=False,
    )
```
